32 devices in a mesh: rows: 8 (over y, x, core), upd: 4 (over z).
Axes of the slice: x: 2, y: 2, z: 4, core: 2. Of those that a mesh axis runs over, the one named last changes fastest.
Arguments:
- tile_factors: bfloat16 [8, 32, 1024, 128], P('rows', 'upd'), may hold values from -6 to 6
- panel_factors: bfloat16 [32, 1024, 128], P('upd', 'rows'), may hold values from -0.1875 to 0.1875
- nonnull: int32 [8, 32], P('rows', 'upd'), may hold values from 0 to 1, as said below
- sketch: float32 [64, 1024], replicated, may hold values from -6 to 6
Outputs:
- update_factors: float32 [8, 1024, 128], P('rows', 'upd')
The draws below stay inside these ranges and needn't reach their ends.
Inputs may be any that keep to these rules, and one draw needn't show every extreme that they name: In every aligned block of 8 update indices the first one is nonnull for every tile row.
All inputs are finite; a program needn't handle non-finite values.
Results may differ from the reference program's by a relative error of at most 0.0003.
Values may be sent and summed in bfloat16 or wider, within the bound.
A program may use at most 64 MiB of HBM per device.

```python
import jax
import jax.numpy as jnp
from jax import lax

B = 1024
R = 64
KD = 8
K = 32
TILES = 8
N_UPD = 4


def draw_nonnull(key, part):
    bits = jax.random.randint(key, (TILES, K), 0, 2).astype(jnp.int32)
    first = jnp.arange(K) % KD == 0
    return jnp.where(first[None, :], 1, bits).astype(jnp.int32)


def block_scale(key, extent, cuts, low, top_value):
    def one(axis_at, parts):
        steps = jax.random.uniform(jax.random.fold_in(jax.random.fold_in(key, 6), axis_at), (parts,), jnp.float32, low / len(cuts), top_value / len(cuts))
        return jnp.repeat(jnp.exp(steps), extent[axis_at] // parts).reshape((-1,) + (1,) * (len(extent) - axis_at - 1))

    factor_of = one(*cuts[0])
    for cut in cuts[1:]:
        factor_of = factor_of * one(*cut)
    return factor_of


def gaussian(key, dims, spread, reach, pieces=(), kind=jnp.bfloat16):
    array = jax.random.normal(key, dims, jnp.float32) * spread
    if len(pieces) > 0:
        array = block_scale(key, dims, pieces, -0.22, 0.18) * array
    return jnp.clip(array, min=-reach, max=reach).astype(kind)


def setup_inputs(seed: int = 0) -> dict:
    streams_of = jax.random.split(jax.random.key(seed), 5)
    return {
        "tile_factors": gaussian(streams_of[0], (TILES, K, B, 2 * R), 1.0, 6.0, ((0, 8), (1, 4))),
        "panel_factors": gaussian(streams_of[1], (K, B, 2 * R), B ** -0.5, 0.1875, ((0, 4), (1, 8))),
        "nonnull": draw_nonnull(jax.random.fold_in(streams_of[4], 71), 0),
        "sketch": gaussian(streams_of[3], (R, B), 1.0, 6.0, (), jnp.float32),
    }


def compress(lefts, rights, sketch):
    hi = lax.Precision.HIGHEST
    proj = jnp.einsum('nbr,sb->nrs', rights, sketch, precision=hi)
    span = jnp.einsum('nbr,nrs->bs', lefts, proj, precision=hi)
    gram = jnp.dot(span.T, span, precision=hi)
    order = gram.shape[0]
    shift = 0.001 * jnp.trace(gram) / order + 1e-20
    gram = gram + shift * jnp.eye(order, dtype=gram.dtype)
    chol = jnp.linalg.cholesky(gram)
    basis = lax.linalg.triangular_solve(chol, span, left_side=False, lower=True, transpose_a=True)
    coef = jnp.einsum('nbr,bs->nrs', lefts, basis, precision=hi)
    image = jnp.einsum('nbr,nrs->bs', rights, coef, precision=hi)
    return (basis, image)

def one_row(tiles, mask, panel, sketch):
    rank = tiles.shape[2] // 2
    own_left = tiles[:, :, :rank].astype(jnp.float32)
    own_right = tiles[:, :, rank:].astype(jnp.float32)
    inner = jnp.einsum('kbr,kbs->krs', own_right, panel[:, :, rank:].astype(jnp.float32))
    lefts = jnp.einsum('kbr,krs->kbs', own_left, inner, precision=lax.Precision.HIGHEST)
    lefts = lefts * mask.astype(jnp.float32)[:, None, None]
    rights = panel[:, :, :rank].astype(jnp.float32)
    lefts = lefts.reshape(N_UPD, KD, B, rank)
    rights = rights.reshape(N_UPD, KD, B, rank)
    basis, image = jax.vmap(lambda a, b: compress(a, b, sketch))(lefts, rights)
    nodes = jnp.concatenate([basis, image], axis=-1)
    count = N_UPD
    while count > 1:
        pairs = nodes.reshape(count // 2, 2, B, 2 * rank)
        basis, image = jax.vmap(lambda p: compress(p[:, :, :rank], p[:, :, rank:], sketch))(pairs)
        nodes = jnp.concatenate([basis, image], axis=-1)
        count = count // 2
    scale = jnp.float32(B) ** 0.5
    return jnp.concatenate([nodes[0, :, :rank] * scale, nodes[0, :, rank:] / scale], axis=-1)

def reference(tile_factors, panel_factors, nonnull, sketch):
    return lax.map(lambda item: one_row(item[0], item[1], panel_factors, sketch), (tile_factors, nonnull))
```

```python
import functools

import jax
import jax.numpy as jnp
from jax import lax
from jax.experimental import pallas as pl
from jax.experimental.pallas import tpu as pltpu
from jax.sharding import PartitionSpec as P

HI = lax.Precision.HIGHEST
F32 = jnp.float32
BF16 = jnp.bfloat16
MESH = pl.DeviceIdType.MESH
NN = (((1,), (0,)), ((), ()))
NT = (((1,), (1,)), ((), ()))
TN = (((0,), (0,)), ((), ()))


def dot(a, b, dims):
    return lax.dot_general(a, b, dims, precision=HI, preferred_element_type=F32)


def dot16(a, b, dims):
    return lax.dot_general(a, b, dims, preferred_element_type=F32)


def split3(x):
    hi = x.astype(BF16)
    rest = x - hi.astype(F32)
    mid = rest.astype(BF16)
    low = (rest - mid.astype(F32)).astype(BF16)
    return jnp.concatenate([hi, mid, low], axis=0)


def sum3(x, rank):
    return x[:rank] + (x[rank : 2 * rank] + x[2 * rank :])


def iotas(rank):
    shape = (rank, 2 * rank)
    return lax.broadcasted_iota(jnp.int32, shape, 0), lax.broadcasted_iota(jnp.int32, shape, 1)


def inverse_factor(gram, rank):
    row, col = iotas(rank)
    diag = col == row + rank
    trace = jnp.sum(jnp.where(diag, gram, 0.0), keepdims=True)
    shift = 0.001 * trace / rank + 1e-20
    m = gram + jnp.where(diag, shift, 0.0) + jnp.where(col == row, 1.0, 0.0)
    for j in range(rank - 1):
        start = (j + 1) // 8 * 8
        pivot_row = m[j : j + 1, :]
        scaled = pivot_row / m[j : j + 1, rank + j : rank + j + 1]
        tail = m[start:]
        factor = tail[:, rank + j : rank + j + 1]
        if (j + 1) % 8:
            factor = jnp.where(row[start:, :1] > j, factor, 0.0)
        tail = tail - factor * scaled
        m = jnp.concatenate([m[:start], tail], axis=0) if start else tail
    pivots = jnp.sum(jnp.where(diag, m, 0.0), axis=1, keepdims=True)
    return (m * lax.rsqrt(pivots))[:, :rank]


def below(x):
    return jnp.concatenate([jnp.zeros_like(x), x], axis=0)


def above(x):
    return jnp.concatenate([x, jnp.zeros_like(x)], axis=0)


def kernel(rows, upd, tile_ref, panel_ref, nonnull_ref, sketch_ref, out_ref,
           panel, inner, proj, *rest):
    levels = upd.bit_length() - 1
    stages, pairs, apairs, ebufs = (rest[v * levels : (v + 1) * levels] for v in range(4))
    chip_send, chip_recv, sib_send, sib_recv, wz_sem, a_sem, e_send, e_recv = rest[4 * levels :]
    count, block, width = panel_ref.shape
    order = tile_ref.shape[2]
    rank = width // 2
    me, z = lax.axis_index("rows"), lax.axis_index("upd")
    chips = rows // 2
    chip, core = me // 2, lax.rem(me, 2)
    sibling = 2 * chip + 1 - core

    def chip_at(offset):
        return lax.rem(chip + offset + chips, chips)

    barrier = pltpu.get_barrier_semaphore()
    peers = [(sibling, z)] + [(2 * chip_at(c) + core, z) for c in range(1, chips)]
    peers += [(me, lax.rem(z + t, upd)) for t in range(1, upd)]
    for peer in peers:
        pl.semaphore_signal(barrier, inc=1, device_id=peer, device_id_type=MESH)
    pl.semaphore_wait(barrier, len(peers))

    def slot(index):
        return panel.at[:, pl.ds(pl.multiple_of(index * block, block), block), :]

    def chip_copy(offset, src, owner):
        return pltpu.make_async_remote_copy(
            src_ref=src, dst_ref=slot(owner), send_sem=chip_send.at[offset],
            recv_sem=chip_recv.at[offset], device_id=(2 * chip_at(offset) + core, z),
            device_id_type=MESH)

    def sib_copy(offset, src, owner):
        return pltpu.make_async_remote_copy(
            src_ref=src, dst_ref=slot(owner), send_sem=sib_send.at[offset],
            recv_sem=sib_recv.at[offset], device_id=(sibling, z), device_id_type=MESH)

    sends = []
    for c in range(1, chips):
        copy = chip_copy(c, panel_ref, me)
        copy.start()
        sends.append(copy)
    copy = sib_copy(0, panel_ref, me)
    copy.start()
    sends.append(copy)
    panel[:, pl.ds(pl.multiple_of(me * block, block), block), :] = panel_ref[...]
    sketch3 = split3(sketch_ref[...])
    for c in range(1, chips):
        source = 2 * chip_at(-c) + core
        chip_copy(c, slot(source), source).wait_recv()
        copy = sib_copy(c, slot(source), source)
        copy.start()
        sends.append(copy)
    for c in range(chips):
        source = 2 * chip_at(-c) + 1 - core
        sib_copy(c, slot(source), source).wait_recv()
    for copy in sends:
        copy.wait_send()

    row, col = iotas(rank)
    left = col < rank
    corner = below(jnp.where(left, 0.0, 1.0))
    span = jnp.zeros((3 * rank, order), F32)
    for k in range(count):
        weight = nonnull_ref[0, k].astype(F32)
        mid = dot16(tile_ref[0, k], panel[k], TN) * (corner * weight)
        inner[k] = mid
        pk = sum3(dot16(sketch3, panel[k], NN), rank)
        proj[k] = pk
        t = pltpu.roll(dot(pltpu.roll(pk, rank, 1), mid, NT), rank, 1)
        span += dot16(split3(t), tile_ref[0, k], NT)
    span = sum3(span, rank)
    linv = inverse_factor(dot(span, below(span), NT), rank)
    basis = dot(linv, span, NN)
    basis3 = split3(basis)
    image = jnp.zeros((3 * rank, order), F32)
    a_own = jnp.zeros((rank, width), F32)
    for k in range(count):
        wu = pltpu.roll(sum3(dot16(basis3, tile_ref[0, k], NN), rank), rank, 1)
        coef = pltpu.roll(dot(wu, inner[k], NN), rank, 1)
        a_own += dot(proj[k], above(coef), NT)
        image += dot16(split3(coef), panel[k], NT)
    image = sum3(image, rank)
    packed = jnp.concatenate([basis, image], axis=0).T
    stages[0][...] = packed.reshape(stages[0].shape)

    for level in range(levels):
        pair, apair, ebuf = pairs[level], apairs[level], ebufs[level]
        stage = stages[level]
        size = 2 << level
        bit = lax.rem(z // (1 << level), 2)
        partner = z + (1 - 2 * bit) * (1 << level)
        wz_copy = pltpu.make_async_remote_copy(
            src_ref=stage.at[:, 1 - bit], dst_ref=pair.at[bit], send_sem=wz_sem.at[level, 0],
            recv_sem=wz_sem.at[level, 1], device_id=(me, partner), device_id_type=MESH)
        wz_copy.start()
        apair[bit] = a_own
        a_copy = pltpu.make_async_remote_copy(
            src_ref=apair.at[bit], dst_ref=apair.at[bit], send_sem=a_sem.at[level, 0],
            recv_sem=a_sem.at[level, 1], device_id=(me, partner), device_id_type=MESH)
        a_copy.start()
        pair[bit] = stage[:, bit]
        a_copy.wait()
        wz_copy.wait()

        part = order // size
        low, high = pair[0].reshape(part, width), pair[1].reshape(part, width)
        a_low, a_high = apair[0], apair[1]
        span = dot(low, a_low, NT) + dot(high, a_high, NT)
        cross_low, cross_high = dot(span, low, TN), dot(span, high, TN)
        place = lax.rem(z, size)
        ebuf[place] = jnp.where(left, cross_low, pltpu.roll(cross_high, rank, 1))
        copies = []
        for t in range(1, size):
            other = z - place + lax.rem(place + t, size)
            copy = pltpu.make_async_remote_copy(
                src_ref=ebuf.at[place], dst_ref=ebuf.at[place], send_sem=e_send.at[level, t],
                recv_sem=e_recv.at[level, t], device_id=(me, other), device_id_type=MESH)
            copy.start()
            copies.append(copy)
        for copy in copies:
            copy.wait()
        cross = ebuf[0]
        for t in range(1, size):
            cross += ebuf[t]
        a_both = a_low + pltpu.roll(a_high, rank, 1)
        linv = inverse_factor(dot(cross, below(a_both), NT), rank)
        coef = dot(linv, cross, NN)
        a_own = dot(a_both, above(coef), NT)
        coef_low = pltpu.roll(jnp.where(left, coef, 0.0), rank, 1)
        coef_high = jnp.where(left, 0.0, coef)
        packed = (dot(span, above(linv), NT) + dot(low, below(coef_low), NT)
                  + dot(high, below(coef_high), NT))
        if level + 1 < levels:
            stages[level + 1][...] = packed.reshape(stages[level + 1].shape)
    scale = jnp.sqrt(F32(order))
    first = lax.broadcasted_iota(jnp.int32, packed.shape, 1) < rank
    out_ref[0] = packed * jnp.where(first, scale, 1.0 / scale)


def solution(mesh):
    rows, upd = mesh.shape["rows"], mesh.shape["upd"]
    levels = upd.bit_length() - 1
    in_specs = (P("rows", "upd", None, None), P("upd", "rows", None), P("rows", "upd"), P())
    out_specs = P("rows", "upd", None)

    def body(tiles, panel, nonnull, sketch):
        count, block, width = panel.shape
        order = tiles.shape[2]
        rank = width // 2
        share = order // upd
        dma = pltpu.SemaphoreType.DMA
        scratch = [
            pltpu.VMEM((count, order, width), BF16),
            pltpu.VMEM((count, width, width), F32),
            pltpu.VMEM((count, rank, width), F32),
        ]
        scratch += [pltpu.VMEM((upd >> v + 1, 2, share, width), F32) for v in range(levels)]
        scratch += [pltpu.VMEM((2, upd >> v + 1, share, width), F32) for v in range(levels)]
        scratch += [pltpu.VMEM((2, rank, width), F32) for v in range(levels)]
        scratch += [pltpu.VMEM((2 << v, rank, width), F32) for v in range(levels)]
        scratch += [dma((rows // 2,))] * 4 + [dma((levels, 2))] * 2 + [dma((levels, upd))] * 2
        vmem = pl.BlockSpec(memory_space=pltpu.VMEM)
        return pl.pallas_call(
            functools.partial(kernel, rows, upd),
            out_shape=jax.ShapeDtypeStruct((1, share, width), F32),
            in_specs=[vmem, vmem, pl.BlockSpec(memory_space=pltpu.SMEM), vmem],
            out_specs=vmem,
            scratch_shapes=scratch,
            compiler_params=pltpu.CompilerParams(
                collective_id=0, has_side_effects=True, vmem_limit_bytes=48 * 1024 * 1024),
        )(tiles, panel, nonnull, sketch)

    return jax.shard_map(body, mesh=mesh, in_specs=in_specs, out_specs=out_specs, check_vma=False)
```

```python
import functools

import jax
import jax.numpy as jnp
from jax import lax
from jax.experimental import pallas as pl
from jax.experimental.pallas import tpu as pltpu
from jax.sharding import PartitionSpec as P

HI = lax.Precision.HIGHEST
GROUP = 4
PARTS = 4
F32 = jnp.float32
BF16 = jnp.bfloat16
MESH = pl.DeviceIdType.MESH
NN = (((1,), (0,)), ((), ()))
NT = (((1,), (1,)), ((), ()))
TN = (((0,), (0,)), ((), ()))


def dot(a, b, dims):
    return lax.dot_general(a, b, dims, precision=HI, preferred_element_type=F32)


def dot16(a, b, dims):
    return lax.dot_general(a, b, dims, preferred_element_type=F32)


def split3(x):
    hi = x.astype(BF16)
    rest = x - hi.astype(F32)
    mid = rest.astype(BF16)
    low = (rest - mid.astype(F32)).astype(BF16)
    return jnp.concatenate([hi, mid, low], axis=0)


def sum3(x, rank):
    return x[:rank] + (x[rank : 2 * rank] + x[2 * rank :])


def iotas(rank):
    shape = (rank, 2 * rank)
    return lax.broadcasted_iota(jnp.int32, shape, 0), lax.broadcasted_iota(jnp.int32, shape, 1)


def inverse_factor(gram, rank):
    row, col = iotas(rank)
    diag = col == row + rank
    trace = jnp.sum(jnp.where(diag, gram, 0.0), keepdims=True)
    shift = 0.001 * trace / rank + 1e-20
    m = gram + jnp.where(diag, shift, 0.0) + jnp.where(col == row, 1.0, 0.0)
    for base in range(0, rank, GROUP):
        start = base // 8 * 8
        tail = m[start:]
        shape = tail.shape
        columns = [
            jnp.broadcast_to(tail[:, rank + j : rank + j + 1], shape)
            for j in range(base, base + GROUP)
        ]
        below_row = row[start:]
        for step in range(GROUP):
            j = base + step
            at = j - start
            column = columns[step]
            factor = jnp.where(below_row > j, column * (1.0 / column[at : at + 1]), 0.0)
            for later in range(step + 1, GROUP):
                columns[later] = columns[later] - factor * columns[later][at : at + 1]
            tail = tail - factor * tail[at : at + 1]
        m = jnp.concatenate([m[:start], tail], axis=0) if start else tail
    pivots = jnp.sum(jnp.where(diag, m, 0.0), axis=1, keepdims=True)
    return (m * lax.rsqrt(pivots))[:, :rank]


def below(x):
    return jnp.concatenate([jnp.zeros_like(x), x], axis=0)


def above(x):
    return jnp.concatenate([x, jnp.zeros_like(x)], axis=0)


def twice(x, rank):
    return jnp.concatenate([x, pltpu.roll(x, rank, 1)], axis=0)


def kernel(rows, upd, tile_hbm, panel_hbm, nonnull_ref, sketch_hbm, out_ref,
           tile, panel, sketch, inner, proj, *rest):
    levels = upd.bit_length() - 1
    stages, zstages, pairs, zpairs, apairs, ebufs = (
        rest[v * levels : (v + 1) * levels] for v in range(6))
    (tile_sem, own_sem, sketch_sem, chip_send, chip_recv, sib_send, sib_recv,
     w_sem, z_sem, a_sem, e_send, e_recv) = rest[6 * levels :]
    count, block, width = panel_hbm.shape
    order = tile_hbm.shape[2]
    rank = width // 2
    step = count // PARTS
    me, z = lax.axis_index("rows"), lax.axis_index("upd")
    chips = rows // 2
    chip, core = me // 2, lax.rem(me, 2)
    sibling = 2 * chip + 1 - core

    sketch_copy = pltpu.make_async_copy(sketch_hbm, sketch, sketch_sem)
    sketch_copy.start()
    tile_copies, own_copies = [], []
    for g in range(PARTS):
        part = pl.ds(g * step, step)
        tile_copies.append(
            pltpu.make_async_copy(tile_hbm.at[0, part], tile.at[part], tile_sem.at[g]))
        tile_copies[g].start()

    def chip_at(offset):
        return lax.rem(chip + offset + chips, chips)

    barrier = pltpu.get_barrier_semaphore()
    peers = [(sibling, z)] + [(2 * chip_at(c) + core, z) for c in range(1, chips)]
    peers += [(me, lax.rem(z + t, upd)) for t in range(1, upd)]
    for peer in peers:
        pl.semaphore_signal(barrier, inc=1, device_id=peer, device_id_type=MESH)
    pl.semaphore_wait(barrier, len(peers))

    def slot(g, index):
        start = pl.multiple_of(index * block, block)
        return panel.at[pl.ds(g * step, step), pl.ds(start, block), :]

    def chip_copy(g, offset, src, owner):
        return pltpu.make_async_remote_copy(
            src_ref=src, dst_ref=slot(g, owner), send_sem=chip_send.at[g, offset],
            recv_sem=chip_recv.at[g, offset], device_id=(2 * chip_at(offset) + core, z),
            device_id_type=MESH)

    def sib_copy(g, offset, src, owner):
        return pltpu.make_async_remote_copy(
            src_ref=src, dst_ref=slot(g, owner), send_sem=sib_send.at[g, offset],
            recv_sem=sib_recv.at[g, offset], device_id=(sibling, z), device_id_type=MESH)

    sends = []
    for g in range(PARTS):
        own = panel_hbm.at[pl.ds(g * step, step)]
        copies = [chip_copy(g, c, own, me) for c in range(1, chips)] + [sib_copy(g, 0, own, me)]
        for copy in copies:
            copy.start()
        sends += copies
        own_copies.append(pltpu.make_async_copy(own, slot(g, me), own_sem.at[g]))
        own_copies[g].start()

    row, col = iotas(rank)
    left = col < rank
    corner = below(jnp.where(left, 0.0, 1.0))
    sketch_copy.wait()
    sketch3 = split3(sketch[...])
    span = jnp.zeros((3 * rank, order), F32)
    for g in range(PARTS):
        for c in range(1, chips):
            source = 2 * chip_at(-c) + core
            chip_copy(g, c, slot(g, source), source).wait_recv()
            copy = sib_copy(g, c, slot(g, source), source)
            copy.start()
            sends.append(copy)
        tile_copies[g].wait()
        own_copies[g].wait()
        for c in range(chips):
            source = 2 * chip_at(-c) + 1 - core
            sib_copy(g, c, slot(g, source), source).wait_recv()
        for k in range(g * step, (g + 1) * step):
            weight = nonnull_ref[0, k].astype(F32)
            mid = dot16(tile[k], panel[k], TN) * (corner * weight)
            inner[k] = mid
            pk = sum3(dot16(sketch3, panel[k], NN), rank)
            proj[k] = pk
            t = pltpu.roll(dot(pltpu.roll(pk, rank, 1), mid, NT), rank, 1)
            span += dot16(split3(t), tile[k], NT)
    span = sum3(span, rank)
    linv = inverse_factor(dot(span, below(span), NT), rank)
    basis = dot(linv, span, NN)

    def fold(x):
        cut = above(x).T.reshape(upd, 2, order // upd // 2, width)
        return cut[:, 0] + pltpu.roll(cut[:, 1], rank, 2)

    def exchange(level, src, dst, sem):
        bit = lax.rem(z // (1 << level), 2)
        partner = z + (1 - 2 * bit) * (1 << level)
        return pltpu.make_async_remote_copy(
            src_ref=src, dst_ref=dst, send_sem=sem.at[level, 0],
            recv_sem=sem.at[level, 1], device_id=(me, partner), device_id_type=MESH)

    def bit_of(level):
        return lax.rem(z // (1 << level), 2)

    def send_half(level, value, stage, pair, sem):
        bit = bit_of(level)
        stage[...] = value.reshape(stage.shape)
        copy = exchange(level, stage.at[:, 1 - bit], pair.at[bit], sem)
        copy.start()
        pair[bit] = stage[:, bit]
        return copy

    def send_sketch(level, value):
        bit = bit_of(level)
        apairs[level][bit] = value
        copy = exchange(level, apairs[level].at[bit], apairs[level].at[bit], a_sem)
        copy.start()
        return copy

    w_copy = send_half(0, fold(basis), stages[0], pairs[0], w_sem)
    basis3 = split3(basis)
    a_own = jnp.zeros((rank, width), F32)
    coefs = []
    for k in range(count):
        wu = pltpu.roll(sum3(dot16(basis3, tile[k], NN), rank), rank, 1)
        coef = pltpu.roll(dot(wu, inner[k], NN), rank, 1)
        a_own += dot(proj[k], above(coef), NT)
        inner[k, :rank] = coef
    a_copy = send_sketch(0, a_own)
    image = jnp.zeros((3 * rank, order), F32)
    for k in range(count):
        image += dot16(split3(inner[k, :rank]), panel[k], NT)
    z_copy = send_half(0, fold(sum3(image, rank)), zstages[0], zpairs[0], z_sem)

    for level in range(levels):
        pair, zpair, ebuf = pairs[level], zpairs[level], ebufs[level]
        size = 2 << level
        a_copy.wait()
        w_copy.wait()
        part = order // size // 2
        low, high = pair[0].reshape(part, width), pair[1].reshape(part, width)
        a_low, a_high = apairs[level][0], apairs[level][1]
        span = dot(low, twice(a_low, rank), NT) + dot(high, twice(a_high, rank), NT)
        cross_low, cross_high = dot(span, low, TN), dot(span, high, TN)
        cross_low = cross_low[:rank] + pltpu.roll(cross_low[rank:], rank, 1)
        cross_high = pltpu.roll(cross_high[:rank], rank, 1) + cross_high[rank:]
        place = lax.rem(z, size)
        ebuf[place] = jnp.where(left, cross_low, cross_high)
        copies = []
        for t in range(1, size):
            other = z - place + lax.rem(place + t, size)
            copy = pltpu.make_async_remote_copy(
                src_ref=ebuf.at[place], dst_ref=ebuf.at[place], send_sem=e_send.at[level, t],
                recv_sem=e_recv.at[level, t], device_id=(me, other), device_id_type=MESH)
            copy.start()
            copies.append(copy)
        for copy in copies:
            copy.wait()
        cross = ebuf[0]
        for t in range(1, size):
            cross += ebuf[t]
        a_both = a_low + pltpu.roll(a_high, rank, 1)
        linv = inverse_factor(dot(cross, below(a_both), NT), rank)
        wide = jnp.concatenate([linv, jnp.zeros_like(linv)], axis=1)
        basis = dot(span, twice(wide, rank), NT)
        coef = dot(linv, cross, NN)
        a_own = dot(a_both, above(coef), NT)
        if level + 1 < levels:
            w_copy = send_half(level + 1, basis, stages[level + 1], pairs[level + 1], w_sem)
            a_copy = send_sketch(level + 1, a_own)
        coef_low = jnp.where(left, coef, 0.0)
        coef_high = pltpu.roll(jnp.where(left, 0.0, coef), rank, 1)
        z_copy.wait()
        image = (dot(zpair[0].reshape(part, width), twice(coef_low, rank), NT)
                 + dot(zpair[1].reshape(part, width), twice(coef_high, rank), NT))
        if level + 1 < levels:
            z_copy = send_half(level + 1, image, zstages[level + 1], zpairs[level + 1], z_sem)
    first = lax.broadcasted_iota(jnp.int32, basis.shape, 1) < rank
    scale = jnp.sqrt(F32(order))
    basis, image = basis * scale, image / scale
    half = basis.shape[0]
    out_ref[0, :half] = jnp.where(first, basis, pltpu.roll(image, rank, 1))
    out_ref[0, half:] = jnp.where(first, pltpu.roll(basis, rank, 1), image)
    for copy in sends:
        copy.wait_send()


def solution(mesh):
    rows, upd = mesh.shape["rows"], mesh.shape["upd"]
    levels = upd.bit_length() - 1
    in_specs = (P("rows", "upd", None, None), P("upd", "rows", None), P("rows", "upd"), P())
    out_specs = P("rows", "upd", None)

    def body(tiles, panel, nonnull, sketch):
        count, block, width = panel.shape
        order = tiles.shape[2]
        rank = width // 2
        share = order // upd
        dma = pltpu.SemaphoreType.DMA
        scratch = [
            pltpu.VMEM((count, order, width), BF16),
            pltpu.VMEM((count, order, width), BF16),
            pltpu.VMEM((rank, order), F32),
            pltpu.VMEM((count, width, width), F32),
            pltpu.VMEM((count, rank, width), F32),
        ]
        scratch += [pltpu.VMEM((upd >> v + 1, 2, share // 2, width), F32) for v in range(levels)] * 2
        scratch += [pltpu.VMEM((2, upd >> v + 1, share // 2, width), F32) for v in range(levels)] * 2
        scratch += [pltpu.VMEM((2, rank, width), F32) for v in range(levels)]
        scratch += [pltpu.VMEM((2 << v, rank, width), F32) for v in range(levels)]
        scratch += [dma((PARTS,)), dma((PARTS,)), dma] + [dma((PARTS, rows // 2))] * 4
        scratch += [dma((levels, 2))] * 3 + [dma((levels, upd))] * 2
        hbm = pl.BlockSpec(memory_space=pl.ANY)
        vmem = pl.BlockSpec(memory_space=pltpu.VMEM)
        return pl.pallas_call(
            functools.partial(kernel, rows, upd),
            out_shape=jax.ShapeDtypeStruct((1, share, width), F32),
            in_specs=[hbm, hbm, pl.BlockSpec(memory_space=pltpu.SMEM), hbm],
            out_specs=vmem,
            scratch_shapes=scratch,
            compiler_params=pltpu.CompilerParams(
                collective_id=0, has_side_effects=True, vmem_limit_bytes=48 * 1024 * 1024),
        )(tiles, panel, nonnull, sketch)

    return jax.shard_map(body, mesh=mesh, in_specs=in_specs, out_specs=out_specs, check_vma=False)
```

```python
import functools

import jax
import jax.numpy as jnp
from jax import lax
from jax.experimental import pallas as pl
from jax.experimental.pallas import tpu as pltpu
from jax.sharding import PartitionSpec as P

HI = lax.Precision.HIGHEST
GROUP = 16
PARTS = 2
F32 = jnp.float32
BF16 = jnp.bfloat16
MESH = pl.DeviceIdType.MESH
NN = (((1,), (0,)), ((), ()))
NT = (((1,), (1,)), ((), ()))
TN = (((0,), (0,)), ((), ()))


def dot(a, b, dims):
    return lax.dot_general(a, b, dims, precision=HI, preferred_element_type=F32)


def dot16(a, b, dims):
    return lax.dot_general(a, b, dims, preferred_element_type=F32)


def split3(x):
    hi = x.astype(BF16)
    rest = x - hi.astype(F32)
    mid = rest.astype(BF16)
    low = (rest - mid.astype(F32)).astype(BF16)
    return jnp.concatenate([hi, mid, low], axis=0)


def sum3(x, rank):
    return x[:rank] + (x[rank : 2 * rank] + x[2 * rank :])


def iotas(rank):
    shape = (rank, 2 * rank)
    return lax.broadcasted_iota(jnp.int32, shape, 0), lax.broadcasted_iota(jnp.int32, shape, 1)


def inverse_factor(gram, rank):
    row, col = iotas(rank)
    diag = col == row + rank
    trace = jnp.sum(jnp.where(diag, gram, 0.0), keepdims=True)
    shift = 0.001 * trace / rank + 1e-20
    m = gram + jnp.where(diag, shift, 0.0) + jnp.where(col == row, 1.0, 0.0)
    for base in range(0, rank, GROUP):
        start = base // 8 * 8
        tail = m[start:]
        shape = tail.shape
        columns = [
            jnp.broadcast_to(tail[:, rank + j : rank + j + 1], shape)
            for j in range(base, base + GROUP)
        ]
        below_row = row[start:]
        for step in range(GROUP):
            j = base + step
            at = j - start
            column = columns[step]
            factor = jnp.where(below_row > j, column * (1.0 / column[at : at + 1]), 0.0)
            for later in range(step + 1, GROUP):
                columns[later] = columns[later] - factor * columns[later][at : at + 1]
            tail = tail - factor * tail[at : at + 1]
        m = jnp.concatenate([m[:start], tail], axis=0) if start else tail
    pivots = jnp.sum(jnp.where(diag, m, 0.0), axis=1, keepdims=True)
    return (m * lax.rsqrt(pivots))[:, :rank]


def below(x):
    return jnp.concatenate([jnp.zeros_like(x), x], axis=0)


def above(x):
    return jnp.concatenate([x, jnp.zeros_like(x)], axis=0)


def twice(x, rank):
    return jnp.concatenate([x, pltpu.roll(x, rank, 1)], axis=0)


def kernel(rows, upd, tile_hbm, panel_hbm, nonnull_ref, sketch_hbm, out_ref,
           tile, panel, sketch, inner, proj, *rest):
    levels = upd.bit_length() - 1
    stages, zstages, pairs, zpairs, apairs, ebufs = (
        rest[v * levels : (v + 1) * levels] for v in range(6))
    (tile_sem, own_sem, sketch_sem, chip_send, chip_recv, sib_send, sib_recv,
     w_sem, z_sem, a_sem, e_send, e_recv) = rest[6 * levels :]
    count, block, width = panel_hbm.shape
    order = tile_hbm.shape[2]
    rank = width // 2
    step = count // PARTS
    me, z = lax.axis_index("rows"), lax.axis_index("upd")
    chips = rows // 2
    chip, core = me // 2, lax.rem(me, 2)
    sibling = 2 * chip + 1 - core

    sketch_copy = pltpu.make_async_copy(sketch_hbm, sketch, sketch_sem)
    sketch_copy.start()
    tile_copies, own_copies = [], []
    for g in range(PARTS):
        part = pl.ds(g * step, step)
        tile_copies.append(
            pltpu.make_async_copy(tile_hbm.at[0, part], tile.at[part], tile_sem.at[g]))
        tile_copies[g].start()

    def chip_at(offset):
        return lax.rem(chip + offset + chips, chips)

    barrier = pltpu.get_barrier_semaphore()
    peers = [(sibling, z)] + [(2 * chip_at(c) + core, z) for c in range(1, chips)]
    peers += [(me, lax.rem(z + t, upd)) for t in range(1, upd)]
    for peer in peers:
        pl.semaphore_signal(barrier, inc=1, device_id=peer, device_id_type=MESH)
    pl.semaphore_wait(barrier, len(peers))

    def slot(g, index):
        start = pl.multiple_of(index * block, block)
        return panel.at[pl.ds(g * step, step), pl.ds(start, block), :]

    def chip_copy(g, offset, src, owner):
        return pltpu.make_async_remote_copy(
            src_ref=src, dst_ref=slot(g, owner), send_sem=chip_send.at[g, offset],
            recv_sem=chip_recv.at[g, offset], device_id=(2 * chip_at(offset) + core, z),
            device_id_type=MESH)

    def sib_copy(g, offset, src, owner):
        return pltpu.make_async_remote_copy(
            src_ref=src, dst_ref=slot(g, owner), send_sem=sib_send.at[g, offset],
            recv_sem=sib_recv.at[g, offset], device_id=(sibling, z), device_id_type=MESH)

    sends = []
    for g in range(PARTS):
        own = panel_hbm.at[pl.ds(g * step, step)]
        copies = [chip_copy(g, c, own, me) for c in range(1, chips)] + [sib_copy(g, 0, own, me)]
        for copy in copies:
            copy.start()
        sends += copies
        own_copies.append(pltpu.make_async_copy(own, slot(g, me), own_sem.at[g]))
        own_copies[g].start()

    row, col = iotas(rank)
    left = col < rank
    corner = below(jnp.where(left, 0.0, 1.0))
    sketch_copy.wait()
    sketch3 = split3(sketch[...])
    span = jnp.zeros((3 * rank, order), F32)
    for g in range(PARTS):
        for c in range(1, chips):
            source = 2 * chip_at(-c) + core
            chip_copy(g, c, slot(g, source), source).wait_recv()
            copy = sib_copy(g, c, slot(g, source), source)
            copy.start()
            sends.append(copy)
        tile_copies[g].wait()
        own_copies[g].wait()
        for c in range(chips):
            source = 2 * chip_at(-c) + 1 - core
            sib_copy(g, c, slot(g, source), source).wait_recv()
        for k in range(g * step, (g + 1) * step):
            weight = nonnull_ref[0, k].astype(F32)
            mid = dot16(tile[k], panel[k], TN) * (corner * weight)
            inner[k] = mid
            pk = sum3(dot16(sketch3, panel[k], NN), rank)
            proj[k] = pk
            t = pltpu.roll(dot(pltpu.roll(pk, rank, 1), mid, NT), rank, 1)
            span += dot16(split3(t), tile[k], NT)
    span = sum3(span, rank)
    linv = inverse_factor(dot(span, below(span), NT), rank)
    basis = dot(linv, span, NN)

    def fold(x):
        cut = above(x).T.reshape(upd, 2, order // upd // 2, width)
        return cut[:, 0] + pltpu.roll(cut[:, 1], rank, 2)

    def exchange(level, src, dst, sem):
        bit = lax.rem(z // (1 << level), 2)
        partner = z + (1 - 2 * bit) * (1 << level)
        return pltpu.make_async_remote_copy(
            src_ref=src, dst_ref=dst, send_sem=sem.at[level, 0],
            recv_sem=sem.at[level, 1], device_id=(me, partner), device_id_type=MESH)

    def bit_of(level):
        return lax.rem(z // (1 << level), 2)

    def send_half(level, value, stage, pair, sem):
        bit = bit_of(level)
        stage[...] = value.reshape(stage.shape)
        copy = exchange(level, stage.at[:, 1 - bit], pair.at[bit], sem)
        copy.start()
        pair[bit] = stage[:, bit]
        return copy

    def send_sketch(level, value):
        bit = bit_of(level)
        apairs[level][bit] = value
        copy = exchange(level, apairs[level].at[bit], apairs[level].at[bit], a_sem)
        copy.start()
        return copy

    w_copy = send_half(0, fold(basis), stages[0], pairs[0], w_sem)
    basis3 = split3(basis)
    a_own = jnp.zeros((rank, width), F32)
    coefs = []
    for k in range(count):
        wu = pltpu.roll(sum3(dot16(basis3, tile[k], NN), rank), rank, 1)
        coef = pltpu.roll(dot(wu, inner[k], NN), rank, 1)
        a_own += dot(proj[k], above(coef), NT)
        inner[k, :rank] = coef
    a_copy = send_sketch(0, a_own)
    image = jnp.zeros((3 * rank, order), F32)
    for k in range(count):
        image += dot16(split3(inner[k, :rank]), panel[k], NT)
    z_copy = send_half(0, fold(sum3(image, rank)), zstages[0], zpairs[0], z_sem)

    for level in range(levels):
        pair, zpair, ebuf = pairs[level], zpairs[level], ebufs[level]
        size = 2 << level
        a_copy.wait()
        w_copy.wait()
        part = order // size // 2
        low, high = pair[0].reshape(part, width), pair[1].reshape(part, width)
        a_low, a_high = apairs[level][0], apairs[level][1]
        span = dot(low, twice(a_low, rank), NT) + dot(high, twice(a_high, rank), NT)
        cross_low, cross_high = dot(span, low, TN), dot(span, high, TN)
        cross_low = cross_low[:rank] + pltpu.roll(cross_low[rank:], rank, 1)
        cross_high = pltpu.roll(cross_high[:rank], rank, 1) + cross_high[rank:]
        place = lax.rem(z, size)
        ebuf[place] = jnp.where(left, cross_low, cross_high)
        copies = []
        for t in range(1, size):
            other = z - place + lax.rem(place + t, size)
            copy = pltpu.make_async_remote_copy(
                src_ref=ebuf.at[place], dst_ref=ebuf.at[place], send_sem=e_send.at[level, t],
                recv_sem=e_recv.at[level, t], device_id=(me, other), device_id_type=MESH)
            copy.start()
            copies.append(copy)
        for copy in copies:
            copy.wait()
        cross = ebuf[0]
        for t in range(1, size):
            cross += ebuf[t]
        a_both = a_low + pltpu.roll(a_high, rank, 1)
        linv = inverse_factor(dot(cross, below(a_both), NT), rank)
        wide = jnp.concatenate([linv, jnp.zeros_like(linv)], axis=1)
        basis = dot(span, twice(wide, rank), NT)
        coef = dot(linv, cross, NN)
        a_own = dot(a_both, above(coef), NT)
        if level + 1 < levels:
            w_copy = send_half(level + 1, basis, stages[level + 1], pairs[level + 1], w_sem)
            a_copy = send_sketch(level + 1, a_own)
        coef_low = jnp.where(left, coef, 0.0)
        coef_high = pltpu.roll(jnp.where(left, 0.0, coef), rank, 1)
        z_copy.wait()
        image = (dot(zpair[0].reshape(part, width), twice(coef_low, rank), NT)
                 + dot(zpair[1].reshape(part, width), twice(coef_high, rank), NT))
        if level + 1 < levels:
            z_copy = send_half(level + 1, image, zstages[level + 1], zpairs[level + 1], z_sem)
    first = lax.broadcasted_iota(jnp.int32, basis.shape, 1) < rank
    scale = jnp.sqrt(F32(order))
    basis, image = basis * scale, image / scale
    half = basis.shape[0]
    out_ref[0, :half] = jnp.where(first, basis, pltpu.roll(image, rank, 1))
    out_ref[0, half:] = jnp.where(first, pltpu.roll(basis, rank, 1), image)
    for copy in sends:
        copy.wait_send()


def solution(mesh):
    rows, upd = mesh.shape["rows"], mesh.shape["upd"]
    levels = upd.bit_length() - 1
    in_specs = (P("rows", "upd", None, None), P("upd", "rows", None), P("rows", "upd"), P())
    out_specs = P("rows", "upd", None)

    def body(tiles, panel, nonnull, sketch):
        count, block, width = panel.shape
        order = tiles.shape[2]
        rank = width // 2
        share = order // upd
        dma = pltpu.SemaphoreType.DMA
        scratch = [
            pltpu.VMEM((count, order, width), BF16),
            pltpu.VMEM((count, order, width), BF16),
            pltpu.VMEM((rank, order), F32),
            pltpu.VMEM((count, width, width), F32),
            pltpu.VMEM((count, rank, width), F32),
        ]
        scratch += [pltpu.VMEM((upd >> v + 1, 2, share // 2, width), F32) for v in range(levels)] * 2
        scratch += [pltpu.VMEM((2, upd >> v + 1, share // 2, width), F32) for v in range(levels)] * 2
        scratch += [pltpu.VMEM((2, rank, width), F32) for v in range(levels)]
        scratch += [pltpu.VMEM((2 << v, rank, width), F32) for v in range(levels)]
        scratch += [dma((PARTS,)), dma((PARTS,)), dma] + [dma((PARTS, rows // 2))] * 4
        scratch += [dma((levels, 2))] * 3 + [dma((levels, upd))] * 2
        hbm = pl.BlockSpec(memory_space=pl.ANY)
        vmem = pl.BlockSpec(memory_space=pltpu.VMEM)
        return pl.pallas_call(
            functools.partial(kernel, rows, upd),
            out_shape=jax.ShapeDtypeStruct((1, share, width), F32),
            in_specs=[hbm, hbm, pl.BlockSpec(memory_space=pltpu.SMEM), hbm],
            out_specs=vmem,
            scratch_shapes=scratch,
            compiler_params=pltpu.CompilerParams(
                collective_id=0, has_side_effects=True, vmem_limit_bytes=48 * 1024 * 1024),
        )(tiles, panel, nonnull, sketch)

    return jax.shard_map(body, mesh=mesh, in_specs=in_specs, out_specs=out_specs, check_vma=False)
```
